512 devices in a mesh: dp: 64 (over z, x), head: 8 (over y, core).
Axes of the slice: x: 4, y: 4, z: 16, core: 2. Of those that a mesh axis runs over, the one named last changes fastest.
Arguments:
- teacher_feat: bfloat16 [16384, 256], P('dp'), may hold values from -8 to 8
- student_feat: bfloat16 [16384, 256], P('dp'), may hold values from -8 to 8
- proto_v: bfloat16 [256, 32768], P('dp', 'head'), may hold values from -8 to 8
Outputs:
- proto_grad: float32 [256, 32768], P('dp', 'head')
- crop_loss: float32 [16384], P('dp')
The draws below stay inside these ranges and needn't reach their ends.
All inputs are finite; a program needn't handle non-finite values.
Results may differ from the reference program's by a relative error of at most 0.00095.
Values may be sent and summed in bfloat16 or wider, within the bound.
No kernel may reach another device: no remote copies, remote signals or barrier semaphores. Data moves between devices by JAX's collectives and lax.ppermute only.
A program may use at most 64 MiB of HBM per device.

```python
import jax
import jax.numpy as jnp
from jax import lax

BOT = 256
PROTOS = 32768
ITERS = 3
CROPS = 16384


def cluster_centers(key):
    return jax.random.normal(key, (32, BOT), jnp.float32)


def shared_labels(key):
    order = jax.random.permutation(jax.random.fold_in(key, 77), 32)
    offsets = jax.random.randint(jax.random.fold_in(key, 78), (CROPS,), 0, 2)
    slots = jnp.arange(CROPS, dtype=jnp.int32) * 32 // CROPS
    return order[(slots + offsets) % 32]


def feature_noise(key, count, scale):
    noise = jax.random.normal(key, (count, BOT), jnp.float32)
    return scale * noise


def draw_teacher_feat(key, part):
    centers = cluster_centers(key)
    labels = shared_labels(key)
    key = jax.random.fold_in(key, 3)
    feats = centers[labels] + feature_noise(key, CROPS, 0.9)
    return jnp.clip(feats, -8.0, 8.0).astype(jnp.bfloat16)


def draw_student_feat(key, part):
    centers = cluster_centers(key)
    labels = shared_labels(key)
    key = jax.random.fold_in(key, 4)
    feats = centers[labels] + feature_noise(key, CROPS, 0.95)
    return jnp.clip(feats, -8.0, 8.0).astype(jnp.bfloat16)


def draw_proto_v(key, part):
    centers = cluster_centers(key)
    key = jax.random.fold_in(key, 5)
    first = jax.random.randint(jax.random.fold_in(key, 1), (PROTOS,), 0, 32)
    second = jax.random.randint(jax.random.fold_in(key, 3), (PROTOS,), 0, 32)
    labels = jnp.minimum(first, second)
    weights = centers[labels] + feature_noise(jax.random.fold_in(key, 2), PROTOS, 1.4)
    return jnp.clip(weights.T, -8.0, 8.0).astype(jnp.bfloat16)


def setup_inputs(seed: int = 0) -> dict:
    key_of = jax.random.split(jax.random.key(seed), 4)
    return {
        "teacher_feat": draw_teacher_feat(jax.random.fold_in(key_of[3], 71), 0),
        "student_feat": draw_student_feat(jax.random.fold_in(key_of[3], 71), 0),
        "proto_v": draw_proto_v(jax.random.fold_in(key_of[3], 71), 0),
    }


teacher_temp = 0.04
student_temp = 0.1

def unit_rows(features):
    widened = features.astype(jnp.float32)
    scale = jnp.sqrt(lax.optimization_barrier(jnp.sum(widened * widened, axis=1, keepdims=True)) + 1e-06)
    return (widened / scale).astype(jnp.bfloat16)

def reference(teacher_feat, student_feat, proto_v):
    block_rows = min(512, CROPS)
    blocks = CROPS // block_rows
    widened = proto_v.astype(jnp.float32)
    col_norms = jnp.sqrt(lax.optimization_barrier(jnp.sum(widened * widened, axis=0)) + 1e-06)
    teacher_unit = lax.optimization_barrier(unit_rows(teacher_feat)).astype(jnp.float32).reshape(blocks, block_rows, BOT)
    student_unit = lax.optimization_barrier(unit_rows(student_feat)).astype(jnp.float32).reshape(blocks, block_rows, BOT)

    def teacher_exp(feat_rows):
        raw_scores = jnp.dot(feat_rows, widened, precision=lax.Precision.HIGHEST)
        return jnp.exp(raw_scores / (col_norms * teacher_temp))

    def first_mass(carried, feat_rows):
        return (carried + lax.optimization_barrier(jnp.sum(teacher_exp(feat_rows), axis=0)), None)
    mass, unused = lax.scan(first_mass, jnp.zeros((PROTOS,), jnp.float32), teacher_unit)
    for repeat in range(ITERS - 1):
        col_scale = 1.0 / (PROTOS * mass)

        def sweep(carried, feat_rows):
            exp_rows = teacher_exp(feat_rows)
            row_scale = 1.0 / (CROPS * lax.optimization_barrier(jnp.sum(exp_rows * col_scale, axis=1)))
            return (carried + lax.optimization_barrier(jnp.sum(exp_rows * row_scale[:, None], axis=0)), None)
        mass, unused = lax.scan(sweep, jnp.zeros((PROTOS,), jnp.float32), teacher_unit)
    col_scale = 1.0 / (PROTOS * mass)

    def final_sweep(carried, feats):
        teacher_rows, student_rows = feats
        exp_rows = teacher_exp(teacher_rows)
        row_scale = 1.0 / (CROPS * lax.optimization_barrier(jnp.sum(exp_rows * col_scale, axis=1)))
        assign = CROPS * (exp_rows * col_scale) * row_scale[:, None]
        student_scores = jnp.dot(student_rows, widened, precision=lax.Precision.HIGHEST) / (col_norms * student_temp)
        spread = jnp.exp(student_scores)
        exp_totals = lax.optimization_barrier(jnp.sum(spread, axis=1))
        crop_loss = jnp.log(exp_totals) - lax.optimization_barrier(jnp.sum(assign * student_scores, axis=1))
        score_grad = ((spread / exp_totals[:, None] - assign) / CROPS).astype(jnp.bfloat16)
        score_grad = lax.optimization_barrier(score_grad).astype(jnp.float32)
        product = lax.dot_general(student_rows, score_grad, (((0,), (0,)), ((), ())), precision=lax.Precision.HIGHEST)
        return (carried + product / student_temp, crop_loss)
    weight_grad, crop_loss = lax.scan(final_sweep, jnp.zeros((BOT, PROTOS), jnp.float32), (teacher_unit, student_unit))
    normed = widened / col_norms
    col_dots = lax.optimization_barrier(jnp.sum(normed * weight_grad, axis=0))
    proto_grad = (weight_grad - normed * col_dots) / col_norms
    return (proto_grad, crop_loss.reshape(CROPS))
```

```python
import jax
import jax.numpy as jnp
from jax import lax
from jax.sharding import Mesh, PartitionSpec as P

ITERS = 3
TEACHER_TEMP = 0.04
STUDENT_TEMP = 0.1
WIRE_SCALE = 32.0

Z = ("h", "l")
ZX = ("h", "l", "x")
XYC = ("x", "y", "c")


def unit_rows(features):
    widened = features.astype(jnp.float32)
    scale = jnp.sqrt(jnp.sum(widened * widened, axis=1, keepdims=True) + 1e-06)
    return (widened / scale).astype(jnp.bfloat16)


def z_sum(values):
    return lax.psum(lax.psum(values, "h"), "l")


def gather_head(values):
    copies = jnp.broadcast_to(values[None], (32,) + values.shape)
    return lax.all_to_all(copies, XYC, 0, 0, tiled=True)


def local(teacher_feat, student_feat, proto_v):
    rows_in, cols_in = proto_v.shape
    nx = lax.axis_size("x")
    nz = lax.axis_size("h") * lax.axis_size("l")
    cols = cols_in // nx
    crop_count = teacher_feat.shape[0] * nz * nx
    proto_count = cols * 32

    units = jnp.concatenate([unit_rows(teacher_feat), unit_rows(student_feat)], axis=1)
    units = lax.all_gather(units, "x", axis=0, tiled=True)
    bot = teacher_feat.shape[1]
    teacher_unit, student_unit = units[:, :bot], units[:, bot:]

    quarters = proto_v.reshape(rows_in, nx, cols).transpose(1, 0, 2)
    quarters = jnp.broadcast_to(quarters[None], (nz, nx, rows_in, cols)).reshape(nz * nx, rows_in, cols)
    protos = lax.all_to_all(quarters, ZX, 0, 0, tiled=True).reshape(nz * nx * rows_in, cols)
    widened = protos.astype(jnp.float32)
    col_norms = jnp.sqrt(jnp.sum(widened * widened, axis=0) + 1e-06)

    teacher_raw = jnp.dot(teacher_unit, protos, preferred_element_type=jnp.float32)
    mass = jnp.exp(teacher_raw / (col_norms * TEACHER_TEMP))
    student_raw = jnp.dot(student_unit, protos, preferred_element_type=jnp.float32)
    student_scores = student_raw / (col_norms * STUDENT_TEMP)
    spread = jnp.exp(student_scores)
    exp_part = jnp.sum(spread, axis=1)

    col_scale = 1.0 / (proto_count * z_sum(jnp.sum(mass, axis=0)))
    got = gather_head(jnp.stack([jnp.sum(mass * col_scale, axis=1), exp_part]))
    row_sum, exp_totals = jnp.sum(got, axis=0)
    row_scale = 1.0 / (crop_count * row_sum)
    col_scale = 1.0 / (proto_count * z_sum(jnp.sum(mass * row_scale[:, None], axis=0)))
    got = gather_head(jnp.stack([jnp.sum(mass * col_scale, axis=1), col_norms]))
    row_scale = 1.0 / (crop_count * jnp.sum(got[:, 0], axis=0))
    me = lax.axis_index(("y", "c"))
    norms = lax.dynamic_index_in_dim(got[:, 1].reshape(nx, 8, cols), me, axis=1, keepdims=False).reshape(-1)
    col_scale = 1.0 / (proto_count * z_sum(jnp.sum(mass * row_scale[:, None], axis=0)))
    weighted = mass * col_scale
    got = gather_head(jnp.stack([jnp.sum(weighted, axis=1), jnp.sum(weighted * student_scores, axis=1)]))
    row_sum, cross = jnp.sum(got, axis=0)
    crop_loss = jnp.log(exp_totals) - cross / row_sum
    score_grad = (spread / exp_totals[:, None] - weighted / row_sum[:, None]).astype(jnp.bfloat16)
    grad = lax.dot_general(
        student_unit, score_grad, (((0,), (0,)), ((), ())), preferred_element_type=jnp.float32
    )
    normed = widened / col_norms
    grad = grad - normed * jnp.sum(normed * grad, axis=0)
    wire = (grad * WIRE_SCALE).astype(jnp.float16).reshape(nz * nx, rows_in, cols)
    wire = lax.all_to_all(wire, ZX, 0, 0, tiled=True)
    total = jnp.sum(wire.astype(jnp.float32).reshape(nz, nx, rows_in, cols), axis=0)
    total = total.transpose(1, 0, 2).reshape(rows_in, cols_in)
    proto_grad = total / (norms * (WIRE_SCALE * STUDENT_TEMP * crop_count))
    loss = lax.dynamic_slice_in_dim(crop_loss, lax.axis_index("x") * teacher_feat.shape[0], teacher_feat.shape[0])
    return proto_grad, loss


def solution(mesh):
    fine = Mesh(mesh.devices.reshape(4, 4, 4, 4, 2), ("h", "l", "x", "y", "c"))
    return jax.shard_map(
        local,
        mesh=fine,
        in_specs=(P(ZX, None), P(ZX, None), P(ZX, ("y", "c"))),
        out_specs=(P(ZX, ("y", "c")), P(ZX)),
        check_vma=False,
    )
```

```python
import functools

import jax
import jax.numpy as jnp
from jax import lax
from jax.experimental import pallas as pl
from jax.experimental.pallas import tpu as pltpu
from jax.sharding import Mesh, PartitionSpec as P

ITERS = 3
TEACHER_TEMP = 0.04
STUDENT_TEMP = 0.1
WIRE_SCALE = 32.0

Z = ("h", "l")
ZX = ("h", "l", "x")
XYC = ("x", "y", "c")


def unit_rows(features):
    widened = features.astype(jnp.float32)
    scale = jnp.sqrt(jnp.sum(widened * widened, axis=1, keepdims=True) + 1e-06)
    return (widened / scale).astype(jnp.bfloat16)


def z_sum(values):
    return lax.psum(lax.psum(values, "h"), "l")


def gather(values, axes, size):
    copies = jnp.broadcast_to(values[None], (size,) + values.shape)
    return lax.all_to_all(copies, axes, 0, 0, tiled=True)


def gather_head(values):
    return gather(values, XYC, 32)


TILE = 256
LANES = 128
VMEM_LIMIT = 24 * 1024 * 1024


def lanes_to_rows(row):
    return jnp.transpose(jnp.broadcast_to(row, (LANES, row.shape[1])))


def row_totals(block):
    part = block[:, :LANES]
    for start in range(LANES, block.shape[1], LANES):
        part = part + block[:, start : start + LANES]
    return jnp.sum(jnp.transpose(part), axis=0, keepdims=True)


def teacher_kernel(unit_ref, proto_ref, mass_ref, col_ref, norm_ref):
    protos = proto_ref[...]
    widened = protos.astype(jnp.float32)
    norms = jnp.sqrt(jnp.sum(widened * widened, axis=0, keepdims=True) + 1e-06)
    norm_ref[...] = norms
    inverse = 1.0 / (norms * TEACHER_TEMP)
    col_ref[...] = jnp.zeros_like(col_ref)

    @pl.loop(0, mass_ref.shape[0], step=TILE)
    def _(start):
        rows = pl.ds(pl.multiple_of(start, TILE), TILE)
        raw = jnp.dot(unit_ref[rows, : protos.shape[0]], proto_ref[...], preferred_element_type=jnp.float32)
        mass = jnp.exp(raw * inverse)
        mass_ref[rows, :] = mass
        col_ref[...] += jnp.sum(mass, axis=0, keepdims=True)


def student_kernel(unit_ref, proto_ref, norm_ref, score_ref, spread_ref, total_ref):
    inverse = 1.0 / (norm_ref[...] * STUDENT_TEMP)
    bot = proto_ref.shape[0]

    @pl.loop(0, score_ref.shape[0], step=TILE)
    def _(start):
        rows = pl.ds(pl.multiple_of(start, TILE), TILE)
        raw = jnp.dot(unit_ref[rows, bot:], proto_ref[...], preferred_element_type=jnp.float32)
        scores = raw * inverse
        score_ref[rows, :] = scores
        spread = jnp.exp(scores)
        spread_ref[rows, :] = spread
        total_ref[:, rows] = row_totals(spread)


def row_kernel(proto_count, mass_ref, col_ref, out_ref):
    scale = 1.0 / (proto_count * col_ref[...])

    @pl.loop(0, mass_ref.shape[0], step=LANES)
    def _(start):
        rows = pl.ds(pl.multiple_of(start, LANES), LANES)
        out_ref[:, rows] = row_totals(mass_ref[rows, :] * scale)


def col_kernel(crop_count, mass_ref, row_ref, out_ref):
    scale = 1.0 / (crop_count * row_ref[...])
    out_ref[...] = jnp.zeros_like(out_ref)
    for start in range(0, mass_ref.shape[0], LANES):
        tall = lanes_to_rows(scale[:, start : start + LANES])
        for lane in range(0, mass_ref.shape[1], LANES):
            block = mass_ref[start : start + LANES, lane : lane + LANES] * tall
            out_ref[:, lane : lane + LANES] += jnp.sum(block, axis=0, keepdims=True)


def cross_kernel(proto_count, mass_ref, score_ref, col_ref, out_ref):
    scale = 1.0 / (proto_count * col_ref[...])

    @pl.loop(0, mass_ref.shape[0], step=LANES)
    def _(start):
        rows = pl.ds(pl.multiple_of(start, LANES), LANES)
        weighted = mass_ref[rows, :] * scale
        out_ref[0:1, rows] = row_totals(weighted)
        out_ref[1:2, rows] = row_totals(weighted * score_ref[rows, :])


def grad_kernel(proto_count, unit_ref, proto_ref, norm_ref, mass_ref, spread_ref, col_ref, row_ref, total_ref, out_ref):
    scale = 1.0 / (proto_count * col_ref[...])
    bot = proto_ref.shape[0]
    by_row = 1.0 / row_ref[...]
    by_total = 1.0 / total_ref[...]
    for start in range(0, mass_ref.shape[0], TILE):
        pieces = []
        for lane in range(0, mass_ref.shape[1], LANES):
            cols = slice(lane, lane + LANES)
            rows = slice(start, start + TILE)
            tall_total = lanes_to_rows(by_total[:, rows])
            tall_row = lanes_to_rows(by_row[:, rows])
            target = mass_ref[rows, cols] * scale[:, cols] * tall_row
            pieces.append((spread_ref[rows, cols] * tall_total - target).astype(jnp.bfloat16))
        part = lax.dot_general(
            unit_ref[start : start + TILE, bot:], jnp.concatenate(pieces, axis=1),
            (((0,), (0,)), ((), ())), preferred_element_type=jnp.float32,
        )
        if start == 0:
            out_ref[...] = part
        else:
            out_ref[...] += part
    normed = proto_ref[...].astype(jnp.float32) / norm_ref[...]
    grad = out_ref[...]
    dots = jnp.sum(normed * grad, axis=0, keepdims=True)
    out_ref[...] = (grad - normed * dots) * WIRE_SCALE


def call(kernel, outs, *args, flops=0, reads=0):
    held = [pltpu.with_memory_space_constraint(a, pltpu.VMEM) if pinned else a for a, pinned in args]
    return pl.pallas_call(
        kernel,
        out_shape=[pltpu.VMEM(shape, jnp.float32) if pinned else jax.ShapeDtypeStruct(shape, jnp.float32) for shape, pinned in outs],
        in_specs=[pl.BlockSpec(memory_space=pltpu.VMEM)] * len(args),
        out_specs=[pl.BlockSpec(memory_space=pltpu.VMEM)] * len(outs),
        compiler_params=pltpu.CompilerParams(vmem_limit_bytes=VMEM_LIMIT),
        cost_estimate=pl.CostEstimate(flops=flops, bytes_accessed=reads, transcendentals=0),
    )(*held)


def local(teacher_feat, student_feat, proto_v):
    rows_in, cols_in = proto_v.shape
    nx = lax.axis_size("x")
    nz = lax.axis_size("h") * lax.axis_size("l")
    cols = cols_in // nx
    crop_count = teacher_feat.shape[0] * nz * nx
    proto_count = cols * 32

    units = jnp.concatenate([unit_rows(teacher_feat), unit_rows(student_feat)], axis=1)
    bot = teacher_feat.shape[1]
    here = lax.axis_index("x")
    crops_in = units.shape[0]
    gathered = jnp.zeros((nx * crops_in, 2 * bot), units.dtype)
    for step in range(nx):
        block = lax.ppermute(units, "x", [((i + step) % nx, i) for i in range(nx)]) if step else units
        gathered = lax.dynamic_update_slice(gathered, block, ((here + step) % nx * crops_in, 0))

    quarters = proto_v.reshape(rows_in, nx, cols).transpose(1, 0, 2)
    quarters = lax.all_to_all(quarters, "x", 0, 0, tiled=True).reshape(nx * rows_in, cols)
    protos = gather(quarters, Z, nz).reshape(nz * nx * rows_in, cols)
    crops = nx * crops_in
    whole, line = (crops, cols), (1, cols)
    share = functools.partial(call, reads=4 * crops * cols)
    mass, sums, norms = share(teacher_kernel, [(whole, True), (line, False), (line, False)], (gathered, False), (protos, False))
    scores, spread, exp_part = share(
        student_kernel, [(whole, True), (whole, True), ((1, crops), False)], (gathered, False), (protos, False), (norms, False)
    )
    by_col = functools.partial(row_kernel, float(proto_count))
    by_row = functools.partial(col_kernel, float(crop_count))
    masses = z_sum(sums)
    (part,) = share(by_col, [((1, crops), False)], (mass, True), (masses, False))
    totals = jnp.sum(gather_head(part), axis=0)
    (sums,) = share(by_row, [(line, False)], (mass, True), (totals, False))
    masses = z_sum(sums)
    (part,) = share(by_col, [((1, crops), False)], (mass, True), (masses, False))
    both = jnp.sum(gather_head(jnp.concatenate([part, exp_part])), axis=0)
    exp_totals = both[1:]
    (sums,) = share(by_row, [(line, False)], (mass, True), (both[:1], False))
    masses = z_sum(sums)
    (part,) = share(
        functools.partial(cross_kernel, float(proto_count)), [((2, crops), False)], (mass, True), (scores, True), (masses, False)
    )
    both = jnp.sum(gather_head(part), axis=0)
    totals, cross = both[:1], both[1:]
    crop_loss = (jnp.log(exp_totals) - cross / totals)[0]
    (grad,) = share(
        functools.partial(grad_kernel, float(proto_count)), [((bot, cols), False)],
        (gathered, False), (protos, False), (norms, False), (mass, True), (spread, True),
        (masses, False), (totals, False), (exp_totals, False),
    )
    wire = grad.astype(jnp.float16).reshape(nz, nx * rows_in, cols)
    wire = lax.all_to_all(wire, Z, 0, 0, tiled=True)
    total = jnp.sum(wire.astype(jnp.float32), axis=0)
    total = total / (norms * (WIRE_SCALE * STUDENT_TEMP * crop_count))
    total = lax.all_to_all(total.reshape(nx, rows_in, cols), "x", 0, 0, tiled=True)
    proto_grad = total.transpose(1, 0, 2).reshape(rows_in, cols_in)
    loss = lax.dynamic_slice_in_dim(crop_loss, lax.axis_index("x") * teacher_feat.shape[0], teacher_feat.shape[0])
    return proto_grad, loss


def solution(mesh):
    fine = Mesh(mesh.devices.reshape(4, 4, 4, 4, 2), ("h", "l", "x", "y", "c"))
    return jax.shard_map(
        local,
        mesh=fine,
        in_specs=(P(ZX, None), P(ZX, None), P(ZX, ("y", "c"))),
        out_specs=(P(ZX, ("y", "c")), P(ZX)),
        check_vma=False,
    )
```

```python
import functools

import jax
import jax.numpy as jnp
from jax import lax
from jax.experimental import pallas as pl
from jax.experimental.pallas import tpu as pltpu
from jax.sharding import Mesh, PartitionSpec as P

ITERS = 3
TEACHER_TEMP = 0.04
STUDENT_TEMP = 0.1
WIRE_SCALE = 32.0

Z = ("h", "l")
ZX = ("h", "l", "x")
XYC = ("x", "y", "c")


def unit_rows(features):
    widened = features.astype(jnp.float32)
    scale = jnp.sqrt(jnp.sum(widened * widened, axis=1, keepdims=True) + 1e-06)
    return (widened / scale).astype(jnp.bfloat16)


def z_sum(values):
    return lax.psum(lax.psum(values, "h"), "l")


def gather(values, axes, size):
    copies = jnp.broadcast_to(values[None], (size,) + values.shape)
    return lax.all_to_all(copies, axes, 0, 0, tiled=True)


def gather_head(values):
    return gather(values, XYC, 32)


TILE = 256
LANES = 128
VMEM_LIMIT = 16 * 1024 * 1024


def lanes_to_rows(row):
    return jnp.transpose(jnp.broadcast_to(row, (LANES, row.shape[1])))


def row_totals(block):
    part = block[:, :LANES]
    for start in range(LANES, block.shape[1], LANES):
        part = part + block[:, start : start + LANES]
    return jnp.sum(jnp.transpose(part), axis=0, keepdims=True)


def masses_of(unit_ref, proto_ref, norm_ref, rows):
    bot = proto_ref.shape[0]
    raw = jnp.dot(unit_ref[rows, :bot], proto_ref[...], preferred_element_type=jnp.float32)
    return jnp.exp(raw * (1.0 / (norm_ref[...] * TEACHER_TEMP)))


def scores_of(unit_ref, proto_ref, norm_ref, rows):
    bot = proto_ref.shape[0]
    raw = jnp.dot(unit_ref[rows, bot:], proto_ref[...], preferred_element_type=jnp.float32)
    return raw * (1.0 / (norm_ref[...] * STUDENT_TEMP))


def teacher_kernel(unit_ref, proto_ref, col_ref, norm_ref):
    widened = proto_ref[...].astype(jnp.float32)
    norm_ref[...] = jnp.sqrt(jnp.sum(widened * widened, axis=0, keepdims=True) + 1e-06)
    col_ref[...] = jnp.zeros_like(col_ref)

    @pl.loop(0, unit_ref.shape[0], step=TILE)
    def _(start):
        rows = pl.ds(pl.multiple_of(start, TILE), TILE)
        col_ref[...] += jnp.sum(masses_of(unit_ref, proto_ref, norm_ref, rows), axis=0, keepdims=True)


def student_kernel(unit_ref, proto_ref, norm_ref, total_ref):
    @pl.loop(0, unit_ref.shape[0], step=TILE)
    def _(start):
        rows = pl.ds(pl.multiple_of(start, TILE), TILE)
        total_ref[:, rows] = row_totals(jnp.exp(scores_of(unit_ref, proto_ref, norm_ref, rows)))


def row_kernel(proto_count, unit_ref, proto_ref, norm_ref, col_ref, out_ref, *mass_ref):
    scale = 1.0 / (proto_count * col_ref[...])

    @pl.loop(0, unit_ref.shape[0], step=TILE)
    def _(start):
        rows = pl.ds(pl.multiple_of(start, TILE), TILE)
        mass = masses_of(unit_ref, proto_ref, norm_ref, rows)
        for ref in mass_ref:
            ref[rows, :] = mass
        out_ref[:, rows] = row_totals(mass * scale)


def col_kernel(crop_count, unit_ref, proto_ref, norm_ref, got_ref, out_ref):
    scale = 1.0 / (crop_count * jnp.sum(got_ref[...], axis=0))
    out_ref[...] = jnp.zeros_like(out_ref)
    for start in range(0, unit_ref.shape[0], TILE):
        tall = lanes_to_rows(scale[:1, start : start + TILE])
        mass = masses_of(unit_ref, proto_ref, norm_ref, slice(start, start + TILE))
        for lane in range(0, mass.shape[1], LANES):
            cols = slice(lane, lane + LANES)
            out_ref[:, cols] += jnp.sum(mass[:, cols] * tall, axis=0, keepdims=True)


def held_col_kernel(crop_count, mass_ref, got_ref, out_ref, both_ref):
    both = jnp.sum(got_ref[...], axis=0)
    both_ref[...] = both
    scale = 1.0 / (crop_count * both)
    out_ref[...] = jnp.zeros_like(out_ref)
    for start in range(0, mass_ref.shape[0], LANES):
        tall = lanes_to_rows(scale[:1, start : start + LANES])
        for lane in range(0, mass_ref.shape[1], LANES):
            block = mass_ref[start : start + LANES, lane : lane + LANES] * tall
            out_ref[:, lane : lane + LANES] += jnp.sum(block, axis=0, keepdims=True)


def cross_kernel(proto_count, unit_ref, proto_ref, norm_ref, col_ref, out_ref, target_ref, score_ref):
    scale = 1.0 / (proto_count * col_ref[...])

    @pl.loop(0, unit_ref.shape[0], step=TILE)
    def _(start):
        rows = pl.ds(pl.multiple_of(start, TILE), TILE)
        scores = scores_of(unit_ref, proto_ref, norm_ref, rows)
        weighted = masses_of(unit_ref, proto_ref, norm_ref, rows) * scale
        score_ref[rows, :] = scores
        target_ref[rows, :] = weighted
        out_ref[0:1, rows] = row_totals(weighted)
        out_ref[1:2, rows] = row_totals(weighted * scores)


def grad_kernel(unit_ref, proto_ref, norm_ref, target_ref, score_ref, got_ref, both_ref, out_ref, loss_ref):
    sums = jnp.sum(got_ref[...], axis=0)
    totals = both_ref[1:2, :]
    loss_ref[...] = jnp.log(totals) - sums[1:2] / sums[0:1]
    bot = proto_ref.shape[0]
    by_row = 1.0 / sums[0:1]
    by_total = 1.0 / totals
    for start in range(0, target_ref.shape[0], TILE):
        rows = slice(start, start + TILE)
        tall_total = lanes_to_rows(by_total[:, rows])
        tall_row = lanes_to_rows(by_row[:, rows])
        pieces = []
        for lane in range(0, target_ref.shape[1], LANES):
            cols = slice(lane, lane + LANES)
            spread = jnp.exp(score_ref[rows, cols]) * tall_total
            pieces.append((spread - target_ref[rows, cols] * tall_row).astype(jnp.bfloat16))
        part = lax.dot_general(
            unit_ref[rows, bot:], jnp.concatenate(pieces, axis=1),
            (((0,), (0,)), ((), ())), preferred_element_type=jnp.float32,
        )
        if start == 0:
            out_ref[...] = part
        else:
            out_ref[...] += part
    normed = proto_ref[...].astype(jnp.float32) / norm_ref[...]
    grad = out_ref[...]
    dots = jnp.sum(normed * grad, axis=0, keepdims=True)
    out_ref[...] = (grad - normed * dots) * WIRE_SCALE


def call(kernel, outs, *args, reads):
    return pl.pallas_call(
        kernel,
        out_shape=[jax.ShapeDtypeStruct(shape, jnp.float32) for shape in outs],
        in_specs=[pl.BlockSpec(memory_space=pltpu.VMEM)] * len(args),
        out_specs=[pl.BlockSpec(memory_space=pltpu.VMEM)] * len(outs),
        compiler_params=pltpu.CompilerParams(vmem_limit_bytes=VMEM_LIMIT),
        cost_estimate=pl.CostEstimate(flops=reads, bytes_accessed=reads, transcendentals=0),
    )(*args)


def local(teacher_feat, student_feat, proto_v):
    rows_in, cols_in = proto_v.shape
    nx = lax.axis_size("x")
    nz = lax.axis_size("h") * lax.axis_size("l")
    cols = cols_in // nx
    crop_count = teacher_feat.shape[0] * nz * nx
    proto_count = cols * 32

    units = jnp.concatenate([unit_rows(teacher_feat), unit_rows(student_feat)], axis=1)
    bot = teacher_feat.shape[1]
    here = lax.axis_index("x")
    crops_in = units.shape[0]
    gathered = jnp.zeros((nx * crops_in, 2 * bot), units.dtype)
    for step in range(nx):
        block = lax.ppermute(units, "x", [((i + step) % nx, i) for i in range(nx)]) if step else units
        gathered = lax.dynamic_update_slice(gathered, block, ((here + step) % nx * crops_in, 0))

    quarters = proto_v.reshape(rows_in, nx, cols).transpose(1, 0, 2)
    quarters = lax.all_to_all(quarters, "x", 0, 0, tiled=True).reshape(nx * rows_in, cols)
    protos = gather(quarters, Z, nz).reshape(nz * nx * rows_in, cols)
    crops = nx * crops_in
    whole, line, tall = (crops, cols), (1, cols), (1, crops)
    share = functools.partial(call, reads=4 * crops * cols)
    by_proto, by_crop = float(proto_count), float(crop_count)
    sums, norms = share(teacher_kernel, [line, line], gathered, protos)
    held = gathered, protos, norms
    (exp_part,) = share(student_kernel, [tall], *held)
    masses = z_sum(sums)
    (part,) = share(functools.partial(row_kernel, by_proto), [tall], *held, masses)
    (sums,) = share(functools.partial(col_kernel, by_crop), [line], *held, gather_head(part))
    masses = z_sum(sums)
    part, mass = share(functools.partial(row_kernel, by_proto), [tall, whole], *held, masses)
    got = gather_head(jnp.concatenate([part, exp_part]))
    sums, both = share(functools.partial(held_col_kernel, by_crop), [line, (2, crops)], mass, got)
    masses = z_sum(sums)
    part, target, scores = share(functools.partial(cross_kernel, by_proto), [(2, crops), whole, whole], *held, masses)
    got = gather_head(part)
    grad, crop_loss = share(grad_kernel, [(bot, cols), tall], *held, target, scores, got, both)
    crop_loss = crop_loss[0]
    wire = grad.astype(jnp.float16).reshape(nz, nx * rows_in, cols)
    wire = lax.all_to_all(wire, Z, 0, 0, tiled=True)
    total = jnp.sum(wire.astype(jnp.float32), axis=0)
    total = total / (norms * (WIRE_SCALE * STUDENT_TEMP * crop_count))
    total = lax.all_to_all(total.reshape(nx, rows_in, cols), "x", 0, 0, tiled=True)
    proto_grad = total.transpose(1, 0, 2).reshape(rows_in, cols_in)
    loss = lax.dynamic_slice_in_dim(crop_loss, lax.axis_index("x") * teacher_feat.shape[0], teacher_feat.shape[0])
    return proto_grad, loss


def solution(mesh):
    fine = Mesh(mesh.devices.reshape(4, 4, 4, 4, 2), ("h", "l", "x", "y", "c"))
    return jax.shard_map(
        local,
        mesh=fine,
        in_specs=(P(ZX, None), P(ZX, None), P(ZX, ("y", "c"))),
        out_specs=(P(ZX, ("y", "c")), P(ZX)),
        check_vma=False,
    )
```

```python
import functools

import jax
import jax.numpy as jnp
from jax import lax
from jax.experimental import pallas as pl
from jax.experimental.pallas import tpu as pltpu
from jax.sharding import Mesh, PartitionSpec as P

ITERS = 3
TEACHER_TEMP = 0.04
STUDENT_TEMP = 0.1
WIRE_SCALE = 32.0

Z = ("h", "l")
ZX = ("h", "l", "x")
XYC = ("x", "y", "c")


def unit_rows(features):
    widened = features.astype(jnp.float32)
    scale = jnp.sqrt(jnp.sum(widened * widened, axis=1, keepdims=True) + 1e-06)
    return (widened / scale).astype(jnp.bfloat16)


def gather(values, axes, size):
    copies = jnp.broadcast_to(values[None], (size,) + values.shape)
    return lax.all_to_all(copies, axes, 0, 0, tiled=True)


def gather_head(values):
    return gather(values, XYC, 32)


TILE = 256
LANES = 128
VMEM_LIMIT = 16 * 1024 * 1024


def lanes_to_rows(row):
    return jnp.transpose(jnp.broadcast_to(row, (LANES, row.shape[1])))


def row_totals(block):
    part = block[:, :LANES]
    for start in range(LANES, block.shape[1], LANES):
        part = part + block[:, start : start + LANES]
    return jnp.sum(jnp.transpose(part), axis=0, keepdims=True)


def masses_of(unit_ref, proto_ref, norm_ref, rows):
    bot = proto_ref.shape[0]
    raw = jnp.dot(unit_ref[rows, :bot], proto_ref[...], preferred_element_type=jnp.float32)
    return jnp.exp(raw * (1.0 / (norm_ref[...] * TEACHER_TEMP)))


def scores_of(unit_ref, proto_ref, norm_ref, rows):
    bot = proto_ref.shape[0]
    raw = jnp.dot(unit_ref[rows, bot:], proto_ref[...], preferred_element_type=jnp.float32)
    return raw * (1.0 / (norm_ref[...] * STUDENT_TEMP))


def teacher_kernel(unit_ref, proto_ref, col_ref, norm_ref, mass_ref):
    widened = proto_ref[...].astype(jnp.float32)
    norm_ref[...] = jnp.sqrt(jnp.sum(widened * widened, axis=0, keepdims=True) + 1e-06)
    col_ref[...] = jnp.zeros_like(col_ref)

    @pl.loop(0, unit_ref.shape[0], step=TILE)
    def _(start):
        rows = pl.ds(pl.multiple_of(start, TILE), TILE)
        mass = masses_of(unit_ref, proto_ref, norm_ref, rows)
        mass_ref[rows, :] = mass
        col_ref[...] += jnp.sum(mass, axis=0, keepdims=True)


def first_row_kernel(proto_count, unit_ref, proto_ref, norm_ref, mass_ref, got_ref, out_ref):
    scale = 1.0 / (proto_count * jnp.sum(got_ref[...], axis=0))

    @pl.loop(0, unit_ref.shape[0], step=TILE)
    def _(start):
        rows = pl.ds(pl.multiple_of(start, TILE), TILE)
        out_ref[0:1, rows] = row_totals(mass_ref[rows, :] * scale)
        out_ref[1:2, rows] = row_totals(jnp.exp(scores_of(unit_ref, proto_ref, norm_ref, rows)))


def row_kernel(proto_count, mass_ref, got_ref, out_ref):
    scale = 1.0 / (proto_count * jnp.sum(got_ref[...], axis=0))

    @pl.loop(0, mass_ref.shape[0], step=LANES)
    def _(start):
        rows = pl.ds(pl.multiple_of(start, LANES), LANES)
        out_ref[:, rows] = row_totals(mass_ref[rows, :] * scale)


def held_col_kernel(crop_count, mass_ref, got_ref, out_ref, both_ref):
    both = jnp.sum(got_ref[...], axis=0)
    both_ref[...] = both
    scale = 1.0 / (crop_count * both)
    out_ref[...] = jnp.zeros_like(out_ref)
    for start in range(0, mass_ref.shape[0], LANES):
        tall = lanes_to_rows(scale[:1, start : start + LANES])
        for lane in range(0, mass_ref.shape[1], LANES):
            block = mass_ref[start : start + LANES, lane : lane + LANES] * tall
            out_ref[:, lane : lane + LANES] += jnp.sum(block, axis=0, keepdims=True)


def cross_kernel(proto_count, unit_ref, proto_ref, norm_ref, mass_ref, got_ref, out_ref, target_ref, score_ref):
    scale = 1.0 / (proto_count * jnp.sum(got_ref[...], axis=0))

    @pl.loop(0, unit_ref.shape[0], step=TILE)
    def _(start):
        rows = pl.ds(pl.multiple_of(start, TILE), TILE)
        scores = scores_of(unit_ref, proto_ref, norm_ref, rows)
        weighted = mass_ref[rows, :] * scale
        score_ref[rows, :] = scores
        target_ref[rows, :] = weighted
        out_ref[0:1, rows] = row_totals(weighted)
        out_ref[1:2, rows] = row_totals(weighted * scores)


def grad_kernel(here_ref, unit_ref, proto_ref, norm_ref, target_ref, score_ref, got_ref, both_ref, out_ref, scale_ref, loss_ref, all_ref):
    sums = jnp.sum(got_ref[...], axis=0)
    totals = both_ref[1:2, :]
    all_ref[...] = jnp.log(totals) - sums[1:2] / sums[0:1]
    block = loss_ref.shape[1]
    loss_ref[...] = all_ref[:, pl.ds(pl.multiple_of(here_ref[0] * block, block), block)]
    bot = proto_ref.shape[0]
    by_row = 1.0 / sums[0:1]
    by_total = 1.0 / totals
    for start in range(0, target_ref.shape[0], TILE):
        rows = slice(start, start + TILE)
        tall_total = lanes_to_rows(by_total[:, rows])
        tall_row = lanes_to_rows(by_row[:, rows])
        pieces = []
        for lane in range(0, target_ref.shape[1], LANES):
            cols = slice(lane, lane + LANES)
            spread = jnp.exp(score_ref[rows, cols]) * tall_total
            pieces.append((spread - target_ref[rows, cols] * tall_row).astype(jnp.bfloat16))
        part = lax.dot_general(
            unit_ref[rows, bot:], jnp.concatenate(pieces, axis=1),
            (((0,), (0,)), ((), ())), preferred_element_type=jnp.float32,
        )
        if start == 0:
            out_ref[...] = part
        else:
            out_ref[...] += part
    normed = proto_ref[...].astype(jnp.float32) / norm_ref[...]
    grad = out_ref[...]
    dots = jnp.sum(normed * grad, axis=0, keepdims=True)
    out_ref[...] = (grad - normed * dots) * WIRE_SCALE
    crop_count = target_ref.shape[0] * 16
    scale_ref[...] = 1.0 / (norm_ref[...] * (WIRE_SCALE * STUDENT_TEMP * crop_count))


def call(kernel, outs, *args, reads, scalar=None, scratch=()):
    vmem = pl.BlockSpec(memory_space=pltpu.VMEM)
    specs = [vmem] * len(args)
    if scalar is not None:
        args, specs = (scalar,) + args, [pl.BlockSpec(memory_space=pltpu.SMEM)] + specs
    return pl.pallas_call(
        kernel,
        out_shape=[jax.ShapeDtypeStruct(shape, jnp.float32) for shape in outs],
        in_specs=specs,
        out_specs=[vmem] * len(outs),
        scratch_shapes=[pltpu.VMEM(shape, jnp.float32) for shape in scratch],
        compiler_params=pltpu.CompilerParams(vmem_limit_bytes=VMEM_LIMIT),
        cost_estimate=pl.CostEstimate(flops=reads, bytes_accessed=reads, transcendentals=0),
    )(*args)


def local(teacher_feat, student_feat, proto_v):
    rows_in, cols_in = proto_v.shape
    nx = lax.axis_size("x")
    nz = lax.axis_size("h") * lax.axis_size("l")
    cols = cols_in // nx
    crop_count = teacher_feat.shape[0] * nz * nx
    proto_count = cols * 32

    units = jnp.concatenate([unit_rows(teacher_feat), unit_rows(student_feat)], axis=1)
    bot = teacher_feat.shape[1]
    here = lax.axis_index("x")
    crops_in = units.shape[0]
    gathered = jnp.zeros((nx * crops_in, 2 * bot), units.dtype)
    for step in range(nx):
        block = lax.ppermute(units, "x", [((i + step) % nx, i) for i in range(nx)]) if step else units
        gathered = lax.dynamic_update_slice(gathered, block, ((here + step) % nx * crops_in, 0))

    quarters = proto_v.reshape(rows_in, nx, cols).transpose(1, 0, 2)
    quarters = lax.all_to_all(quarters, "x", 0, 0, tiled=True).reshape(nx * rows_in, cols)
    protos = gather(quarters, Z, nz).reshape(nz * nx * rows_in, cols)
    crops = nx * crops_in
    whole, line, tall = (crops, cols), (1, cols), (1, crops)
    share = functools.partial(call, reads=4 * crops * cols)
    by_proto, by_crop = float(proto_count), float(crop_count)
    sums, norms, mass = share(teacher_kernel, [line, line, whole], gathered, protos)
    held = gathered, protos, norms
    to_rows, to_cols = functools.partial(row_kernel, by_proto), functools.partial(held_col_kernel, by_crop)
    (part,) = share(functools.partial(first_row_kernel, by_proto), [(2, crops)], *held, mass, gather(sums, Z, nz))
    sums, both = share(to_cols, [line, (2, crops)], mass, gather_head(part))
    (part,) = share(to_rows, [tall], mass, gather(sums, Z, nz))
    sums, _ = share(to_cols, [line, tall], mass, gather_head(part))
    part, target, scores = share(
        functools.partial(cross_kernel, by_proto), [(2, crops), whole, whole], *held, mass, gather(sums, Z, nz)
    )
    got = gather_head(part)
    grad, scale, loss = share(
        grad_kernel, [(bot, cols), line, (1, crops_in)], *held, target, scores, got, both,
        scalar=here.astype(jnp.int32).reshape(1), scratch=[tall],
    )
    wire = grad.astype(jnp.float16).reshape(nz, nx * rows_in, cols)
    wire = lax.all_to_all(wire, Z, 0, 0, tiled=True)
    total = jnp.sum(wire.astype(jnp.float32), axis=0)
    total = total * scale
    total = lax.all_to_all(total.reshape(nx, rows_in, cols), "x", 0, 0, tiled=True)
    proto_grad = total.transpose(1, 0, 2).reshape(rows_in, cols_in)
    return proto_grad, loss[0]


def solution(mesh):
    fine = Mesh(mesh.devices.reshape(4, 4, 4, 4, 2), ("h", "l", "x", "y", "c"))
    return jax.shard_map(
        local,
        mesh=fine,
        in_specs=(P(ZX, None), P(ZX, None), P(ZX, ("y", "c"))),
        out_specs=(P(ZX, ("y", "c")), P(ZX)),
        check_vma=False,
    )
```

```python
import functools

import jax
import jax.numpy as jnp
from jax import lax
from jax.experimental import pallas as pl
from jax.experimental.pallas import tpu as pltpu
from jax.sharding import Mesh, PartitionSpec as P

ITERS = 3
TEACHER_TEMP = 0.04
STUDENT_TEMP = 0.1
WIRE_SCALE = 32.0

Z = ("h", "l")
ZX = ("h", "l", "x")
XYC = ("x", "y", "c")


def gather(values, axes, size):
    copies = jnp.broadcast_to(values[None], (size,) + values.shape)
    return lax.all_to_all(copies, axes, 0, 0, tiled=True)


def gather_head(values):
    return gather(values, XYC, 32)


TILE = 256
LANES = 128
VMEM_LIMIT = 16 * 1024 * 1024


def lanes_to_rows(row):
    return jnp.transpose(jnp.broadcast_to(row, (LANES, row.shape[1])))


def row_totals(block):
    part = block[:, :LANES]
    for start in range(LANES, block.shape[1], LANES):
        part = part + block[:, start : start + LANES]
    return jnp.sum(jnp.transpose(part), axis=0, keepdims=True)


def unit_kernel(feat_ref, unit_ref):
    bot = feat_ref.shape[1] // 2
    for half in (slice(0, bot), slice(bot, 2 * bot)):
        widened = feat_ref[:, half].astype(jnp.float32)
        scale = jnp.sqrt(jnp.sum(widened * widened, axis=1, keepdims=True) + 1e-06)
        unit_ref[:, half] = (widened / scale).astype(jnp.bfloat16)


def fold(row):
    return jnp.concatenate([row[:, i : i + LANES] for i in range(0, row.shape[1], LANES)], axis=0)


def unfold(block):
    return jnp.concatenate([block[i : i + 1, :] for i in range(block.shape[0])], axis=1)


def store_totals(out_ref, first, block):
    for i in range(TILE // LANES):
        out_ref[pl.ds(first + i, 1), :] = row_totals(block[i * LANES : (i + 1) * LANES, :])


def masses_of(unit_ref, proto_ref, norm_ref, rows):
    bot = proto_ref.shape[0]
    raw = jnp.dot(unit_ref[rows, :bot], proto_ref[...], preferred_element_type=jnp.float32)
    return jnp.exp(raw * (1.0 / (norm_ref[...] * TEACHER_TEMP)))


def scores_of(unit_ref, proto_ref, norm_ref, rows):
    bot = proto_ref.shape[0]
    raw = jnp.dot(unit_ref[rows, bot:], proto_ref[...], preferred_element_type=jnp.float32)
    return raw * (1.0 / (norm_ref[...] * STUDENT_TEMP))


def teacher_kernel(unit_ref, proto_ref, col_ref, norm_ref, mass_ref):
    widened = proto_ref[...].astype(jnp.float32)
    norm_ref[...] = jnp.sqrt(jnp.sum(widened * widened, axis=0, keepdims=True) + 1e-06)

    def step(i, sums):
        rows = pl.ds(pl.multiple_of(i * TILE, TILE), TILE)
        mass = masses_of(unit_ref, proto_ref, norm_ref, rows)
        mass_ref[rows, :] = mass
        return sums + jnp.sum(mass, axis=0, keepdims=True)

    steps = unit_ref.shape[0] // TILE
    col_ref[...] = fold(lax.fori_loop(0, steps, step, jnp.zeros(norm_ref.shape, jnp.float32)))


def first_row_kernel(proto_count, unit_ref, proto_ref, norm_ref, mass_ref, got_ref, out_ref, score_ref, spread_ref):
    scale = unfold(1.0 / (proto_count * jnp.sum(got_ref[...], axis=0)))
    half = out_ref.shape[0] // 2

    @pl.loop(0, unit_ref.shape[0] // TILE)
    def _(i):
        rows = pl.ds(pl.multiple_of(i * TILE, TILE), TILE)
        first = i * (TILE // LANES)
        store_totals(out_ref, first, mass_ref[rows, :] * scale)
        scores = scores_of(unit_ref, proto_ref, norm_ref, rows)
        spread = jnp.exp(scores)
        score_ref[rows, :] = scores
        spread_ref[rows, :] = spread
        store_totals(out_ref, half + first, spread)


def row_kernel(proto_count, mass_ref, got_ref, out_ref):
    scale = unfold(1.0 / (proto_count * jnp.sum(got_ref[...], axis=0)))

    @pl.loop(0, mass_ref.shape[0] // TILE)
    def _(i):
        rows = pl.ds(pl.multiple_of(i * TILE, TILE), TILE)
        store_totals(out_ref, i * (TILE // LANES), mass_ref[rows, :] * scale)


def col_sums(scale, mass_ref):
    cols = []
    tall = [lanes_to_rows(scale[i : i + 1, :]) for i in range(scale.shape[0])]
    for lane in range(0, mass_ref.shape[1], LANES):
        total = jnp.zeros((1, LANES), jnp.float32)
        for i, factor in enumerate(tall):
            block = mass_ref[i * LANES : (i + 1) * LANES, lane : lane + LANES] * factor
            total = total + jnp.sum(block, axis=0, keepdims=True)
        cols.append(total)
    return jnp.concatenate(cols, axis=0)


def first_col_kernel(crop_count, mass_ref, got_ref, out_ref, total_ref):
    both = jnp.sum(got_ref[...], axis=0)
    half = both.shape[0] // 2
    total_ref[...] = both[half:]
    out_ref[...] = col_sums(1.0 / (crop_count * both[:half]), mass_ref)


def col_kernel(crop_count, mass_ref, got_ref, out_ref):
    out_ref[...] = col_sums(1.0 / (crop_count * jnp.sum(got_ref[...], axis=0)), mass_ref)


def cross_kernel(proto_count, mass_ref, score_ref, got_ref, out_ref, scale_ref):
    scale = unfold(1.0 / (proto_count * jnp.sum(got_ref[...], axis=0)))
    scale_ref[...] = scale
    half = out_ref.shape[0] // 2

    @pl.loop(0, mass_ref.shape[0] // TILE)
    def _(i):
        rows = pl.ds(pl.multiple_of(i * TILE, TILE), TILE)
        first = i * (TILE // LANES)
        weighted = mass_ref[rows, :] * scale
        store_totals(out_ref, first, weighted)
        store_totals(out_ref, half + first, weighted * score_ref[rows, :])


def grad_kernel(crop_count, here_ref, unit_ref, proto_ref, norm_ref, mass_ref, spread_ref, scale_ref, got_ref, total_ref, out_ref, back_ref, loss_ref, all_ref):
    sums = jnp.sum(got_ref[...], axis=0)
    totals = total_ref[...]
    half = totals.shape[0]
    all_ref[...] = jnp.log(totals) - sums[half:] / sums[:half]
    block = loss_ref.shape[0]
    loss_ref[...] = all_ref[pl.ds(here_ref[0] * block, block), :]
    bot = proto_ref.shape[0]
    by_row = 1.0 / sums[:half]
    by_total = 1.0 / totals
    grad = jnp.zeros(out_ref.shape, jnp.float32)
    for start in range(0, mass_ref.shape[0], TILE):
        tiles = []
        for top in range(start, start + TILE, LANES):
            rows, i = slice(top, top + LANES), top // LANES
            tall_total = lanes_to_rows(by_total[i : i + 1, :])
            tall_row = lanes_to_rows(by_row[i : i + 1, :])
            pieces = []
            for lane in range(0, mass_ref.shape[1], LANES):
                cols = slice(lane, lane + LANES)
                target = mass_ref[rows, cols] * scale_ref[:, cols] * tall_row
                pieces.append((spread_ref[rows, cols] * tall_total - target).astype(jnp.bfloat16))
            tiles.append(jnp.concatenate(pieces, axis=1))
        grad = grad + lax.dot_general(
            unit_ref[start : start + TILE, bot:], jnp.concatenate(tiles, axis=0),
            (((0,), (0,)), ((), ())), preferred_element_type=jnp.float32,
        )
    normed = proto_ref[...].astype(jnp.float32) / norm_ref[...]
    dots = jnp.sum(normed * grad, axis=0, keepdims=True)
    out_ref[...] = (grad - normed * dots) * WIRE_SCALE
    back_ref[...] = 1.0 / (norm_ref[...] * (WIRE_SCALE * STUDENT_TEMP * crop_count))


def call(kernel, outs, *args, reads, scalar=None, scratch=(), dtype=jnp.float32):
    vmem = pl.BlockSpec(memory_space=pltpu.VMEM)
    specs = [vmem] * len(args)
    if scalar is not None:
        args, specs = (scalar,) + args, [pl.BlockSpec(memory_space=pltpu.SMEM)] + specs
    return pl.pallas_call(
        kernel,
        out_shape=[jax.ShapeDtypeStruct(shape, dtype) for shape in outs],
        in_specs=specs,
        out_specs=[vmem] * len(outs),
        scratch_shapes=[pltpu.VMEM(shape, jnp.float32) for shape in scratch],
        compiler_params=pltpu.CompilerParams(vmem_limit_bytes=VMEM_LIMIT),
        cost_estimate=pl.CostEstimate(flops=reads, bytes_accessed=reads, transcendentals=0),
    )(*args)


def local(teacher_feat, student_feat, proto_v):
    rows_in, cols_in = proto_v.shape
    nx = lax.axis_size("x")
    nz = lax.axis_size("h") * lax.axis_size("l")
    cols = cols_in // nx
    crop_count = teacher_feat.shape[0] * nz * nx
    proto_count = cols * 32

    crops_in, bot = teacher_feat.shape
    here = lax.axis_index("x")
    feats = jnp.concatenate([teacher_feat, student_feat], axis=1)
    (units,) = call(unit_kernel, [feats.shape], feats, reads=4 * crops_in * bot, dtype=jnp.bfloat16)
    gathered = jnp.zeros((nx * crops_in, 2 * bot), units.dtype)
    for step in range(nx):
        block = lax.ppermute(units, "x", [((i + step) % nx, i) for i in range(nx)]) if step else units
        gathered = lax.dynamic_update_slice(gathered, block, ((here + step) % nx * crops_in, 0))

    quarters = proto_v.reshape(rows_in, nx, cols).transpose(1, 0, 2)
    quarters = lax.all_to_all(quarters, "x", 0, 0, tiled=True).reshape(nx * rows_in, cols)
    protos = gather(quarters, Z, nz).reshape(bot, cols)

    crops = nx * crops_in
    whole, line = (crops, cols), (1, cols)
    col_fold, row_fold, row_pair = (cols // LANES, LANES), (crops // LANES, LANES), (2 * crops // LANES, LANES)
    share = functools.partial(call, reads=4 * crops * cols)
    by_proto, by_crop = float(proto_count), float(crop_count)
    sums, norms, mass = share(teacher_kernel, [col_fold, line, whole], gathered, protos)
    held = gathered, protos, norms
    part, scores, spread = share(
        functools.partial(first_row_kernel, by_proto), [row_pair, whole, whole], *held, mass, gather(sums, Z, nz)
    )
    sums, totals = share(functools.partial(first_col_kernel, by_crop), [col_fold, row_fold], mass, gather_head(part))
    (part,) = share(functools.partial(row_kernel, by_proto), [row_fold], mass, gather(sums, Z, nz))
    (sums,) = share(functools.partial(col_kernel, by_crop), [col_fold], mass, gather_head(part))
    part, scale = share(functools.partial(cross_kernel, by_proto), [row_pair, line], mass, scores, gather(sums, Z, nz))
    grad, back, loss = share(
        functools.partial(grad_kernel, by_crop), [(bot, cols), line, (crops_in // LANES, LANES)], *held, mass, spread, scale, gather_head(part), totals,
        scalar=here.astype(jnp.int32).reshape(1), scratch=[row_fold],
    )
    wire = lax.all_to_all(grad.astype(jnp.float16).reshape(nz, nx * rows_in, cols), Z, 0, 0, tiled=True)
    total = jnp.sum(wire.astype(jnp.float32), axis=0) * back
    total = lax.all_to_all(total.reshape(nx, rows_in, cols), "x", 0, 0, tiled=True)
    return total.transpose(1, 0, 2).reshape(rows_in, cols_in), loss.reshape(crops_in)


def solution(mesh):
    fine = Mesh(mesh.devices.reshape(4, 4, 4, 4, 2), ("h", "l", "x", "y", "c"))
    return jax.shard_map(
        local,
        mesh=fine,
        in_specs=(P(ZX, None), P(ZX, None), P(ZX, ("y", "c"))),
        out_specs=(P(ZX, ("y", "c")), P(ZX)),
        check_vma=False,
    )
```

```python
import functools

import jax
import jax.numpy as jnp
from jax import lax
from jax.experimental import pallas as pl
from jax.experimental.pallas import tpu as pltpu
from jax.sharding import Mesh, PartitionSpec as P

ITERS = 3
TEACHER_TEMP = 0.04
STUDENT_TEMP = 0.1
WIRE_SCALE = 32.0

Z = ("h", "l")
ZX = ("h", "l", "x")
XYC = ("x", "y", "c")


def gather(values, axes, size):
    copies = jnp.broadcast_to(values[None], (size,) + values.shape)
    return lax.all_to_all(copies, axes, 0, 0, tiled=True)


def gather_head(values):
    return gather(values, XYC, 32)


TILE = 256
LANES = 128
VMEM_LIMIT = 16 * 1024 * 1024


def lanes_to_rows(row):
    return jnp.transpose(jnp.broadcast_to(row, (LANES, row.shape[1])))


def row_totals(block):
    part = block[:, :LANES]
    for start in range(LANES, block.shape[1], LANES):
        part = part + block[:, start : start + LANES]
    return jnp.sum(jnp.transpose(part), axis=0, keepdims=True)


def unit_kernel(feat_ref, unit_ref):
    bot = feat_ref.shape[1] // 2
    for half in (slice(0, bot), slice(bot, 2 * bot)):
        widened = feat_ref[:, half].astype(jnp.float32)
        scale = jnp.sqrt(jnp.sum(widened * widened, axis=1, keepdims=True) + 1e-06)
        unit_ref[:, half] = (widened / scale).astype(jnp.bfloat16)


def fold(row):
    return jnp.concatenate([row[:, i : i + LANES] for i in range(0, row.shape[1], LANES)], axis=0)


def unfold(block):
    return jnp.concatenate([block[i : i + 1, :] for i in range(block.shape[0])], axis=1)


def put_totals(held, first, block):
    row = lax.broadcasted_iota(jnp.int32, held.shape, 0)
    for i in range(TILE // LANES):
        held = jnp.where(row == first + i, row_totals(block[i * LANES : (i + 1) * LANES, :]), held)
    return held


def over_tiles(step, ref, rows):
    def body(i, held):
        tile = pl.ds(pl.multiple_of(i * TILE, TILE), TILE)
        return step(i * (TILE // LANES), tile, held)

    return lax.fori_loop(0, ref.shape[0] // TILE, body, jnp.zeros((rows, LANES), jnp.float32))


def masses_of(unit_ref, proto_ref, norm_ref, rows):
    bot = proto_ref.shape[0]
    raw = jnp.dot(unit_ref[rows, :bot], proto_ref[...], preferred_element_type=jnp.float32)
    return jnp.exp(raw * (1.0 / (norm_ref[...] * TEACHER_TEMP)))


def scores_of(unit_ref, proto_ref, norm_ref, rows):
    bot = proto_ref.shape[0]
    raw = jnp.dot(unit_ref[rows, bot:], proto_ref[...], preferred_element_type=jnp.float32)
    return raw * (1.0 / (norm_ref[...] * STUDENT_TEMP))


def teacher_kernel(unit_ref, proto_ref, col_ref, norm_ref, mass_ref):
    widened = proto_ref[...].astype(jnp.float32)
    norm_ref[...] = jnp.sqrt(jnp.sum(widened * widened, axis=0, keepdims=True) + 1e-06)

    def step(i, sums):
        rows = pl.ds(pl.multiple_of(i * TILE, TILE), TILE)
        mass = masses_of(unit_ref, proto_ref, norm_ref, rows)
        mass_ref[rows, :] = mass
        return sums + jnp.sum(mass, axis=0, keepdims=True)

    steps = unit_ref.shape[0] // TILE
    col_ref[...] = fold(lax.fori_loop(0, steps, step, jnp.zeros(norm_ref.shape, jnp.float32)))


def first_row_kernel(proto_count, unit_ref, proto_ref, norm_ref, mass_ref, got_ref, out_ref, score_ref, spread_ref):
    scale = unfold(1.0 / (proto_count * jnp.sum(got_ref[...], axis=0)))
    half = out_ref.shape[0] // 2

    def step(first, rows, held):
        scores = scores_of(unit_ref, proto_ref, norm_ref, rows)
        spread = jnp.exp(scores)
        score_ref[rows, :] = scores
        spread_ref[rows, :] = spread
        held = put_totals(held, first, mass_ref[rows, :] * scale)
        return put_totals(held, half + first, spread)

    out_ref[...] = over_tiles(step, mass_ref, 2 * half)


def row_kernel(proto_count, mass_ref, got_ref, out_ref):
    scale = unfold(1.0 / (proto_count * jnp.sum(got_ref[...], axis=0)))

    def step(first, rows, held):
        return put_totals(held, first, mass_ref[rows, :] * scale)

    out_ref[...] = over_tiles(step, mass_ref, out_ref.shape[0])


def col_sums(scale, mass_ref):
    cols = []
    tall = [lanes_to_rows(scale[i : i + 1, :]) for i in range(scale.shape[0])]
    for lane in range(0, mass_ref.shape[1], LANES):
        total = jnp.zeros((1, LANES), jnp.float32)
        for i, factor in enumerate(tall):
            block = mass_ref[i * LANES : (i + 1) * LANES, lane : lane + LANES] * factor
            total = total + jnp.sum(block, axis=0, keepdims=True)
        cols.append(total)
    return jnp.concatenate(cols, axis=0)


def first_col_kernel(crop_count, mass_ref, got_ref, out_ref, total_ref):
    both = jnp.sum(got_ref[...], axis=0)
    half = both.shape[0] // 2
    total_ref[...] = both[half:]
    out_ref[...] = col_sums(1.0 / (crop_count * both[:half]), mass_ref)


def col_kernel(crop_count, mass_ref, got_ref, out_ref):
    out_ref[...] = col_sums(1.0 / (crop_count * jnp.sum(got_ref[...], axis=0)), mass_ref)


def cross_kernel(proto_count, mass_ref, score_ref, got_ref, out_ref, scale_ref):
    scale = unfold(1.0 / (proto_count * jnp.sum(got_ref[...], axis=0)))
    scale_ref[...] = scale
    half = out_ref.shape[0] // 2

    def step(first, rows, held):
        weighted = mass_ref[rows, :] * scale
        held = put_totals(held, first, weighted)
        return put_totals(held, half + first, weighted * score_ref[rows, :])

    out_ref[...] = over_tiles(step, mass_ref, 2 * half)


def grad_kernel(crop_count, here_ref, unit_ref, proto_ref, norm_ref, mass_ref, spread_ref, scale_ref, got_ref, total_ref, out_ref, back_ref, loss_ref):
    sums = jnp.sum(got_ref[...], axis=0)
    totals = total_ref[...]
    half = totals.shape[0]
    losses = jnp.log(totals) - sums[half:] / sums[:half]
    block = loss_ref.shape[0]
    loss = losses[:block]
    for x in range(1, half // block):
        loss = jnp.where(here_ref[0] == x, losses[x * block : (x + 1) * block], loss)
    loss_ref[...] = loss
    bot = proto_ref.shape[0]
    by_row = 1.0 / sums[:half]
    by_total = 1.0 / totals
    grad = jnp.zeros(out_ref.shape, jnp.float32)
    for start in range(0, mass_ref.shape[0], TILE):
        tiles = []
        for top in range(start, start + TILE, LANES):
            rows, i = slice(top, top + LANES), top // LANES
            tall_total = lanes_to_rows(by_total[i : i + 1, :])
            tall_row = lanes_to_rows(by_row[i : i + 1, :])
            pieces = []
            for lane in range(0, mass_ref.shape[1], LANES):
                cols = slice(lane, lane + LANES)
                target = mass_ref[rows, cols] * scale_ref[:, cols] * tall_row
                pieces.append((spread_ref[rows, cols] * tall_total - target).astype(jnp.bfloat16))
            tiles.append(jnp.concatenate(pieces, axis=1))
        grad = grad + lax.dot_general(
            unit_ref[start : start + TILE, bot:], jnp.concatenate(tiles, axis=0),
            (((0,), (0,)), ((), ())), preferred_element_type=jnp.float32,
        )
    normed = proto_ref[...].astype(jnp.float32) / norm_ref[...]
    dots = jnp.sum(normed * grad, axis=0, keepdims=True)
    out_ref[...] = (grad - normed * dots) * WIRE_SCALE
    back_ref[...] = 1.0 / (norm_ref[...] * (WIRE_SCALE * STUDENT_TEMP * crop_count))


def call(kernel, outs, *args, reads, scalar=None, dtype=jnp.float32):
    vmem = pl.BlockSpec(memory_space=pltpu.VMEM)
    specs = [vmem] * len(args)
    if scalar is not None:
        args, specs = (scalar,) + args, [pl.BlockSpec(memory_space=pltpu.SMEM)] + specs
    return pl.pallas_call(
        kernel,
        out_shape=[jax.ShapeDtypeStruct(shape, dtype) for shape in outs],
        in_specs=specs,
        out_specs=[vmem] * len(outs),
        compiler_params=pltpu.CompilerParams(vmem_limit_bytes=VMEM_LIMIT),
        cost_estimate=pl.CostEstimate(flops=reads, bytes_accessed=reads, transcendentals=0),
    )(*args)


def local(teacher_feat, student_feat, proto_v):
    rows_in, cols_in = proto_v.shape
    nx = lax.axis_size("x")
    nz = lax.axis_size("h") * lax.axis_size("l")
    cols = cols_in // nx
    crop_count = teacher_feat.shape[0] * nz * nx
    proto_count = cols * 32

    crops_in, bot = teacher_feat.shape
    here = lax.axis_index("x")
    feats = jnp.concatenate([teacher_feat, student_feat], axis=1)
    (units,) = call(unit_kernel, [feats.shape], feats, reads=4 * crops_in * bot, dtype=jnp.bfloat16)
    gathered = jnp.zeros((nx * crops_in, 2 * bot), units.dtype)
    for step in range(nx):
        block = lax.ppermute(units, "x", [((i + step) % nx, i) for i in range(nx)]) if step else units
        gathered = lax.dynamic_update_slice(gathered, block, ((here + step) % nx * crops_in, 0))

    quarters = proto_v.reshape(rows_in, nx, cols).transpose(1, 0, 2)
    quarters = lax.all_to_all(quarters, "x", 0, 0, tiled=True).reshape(nx * rows_in, cols)
    protos = gather(quarters, Z, nz).reshape(bot, cols)

    crops = nx * crops_in
    whole, line = (crops, cols), (1, cols)
    col_fold, row_fold, row_pair = (cols // LANES, LANES), (crops // LANES, LANES), (2 * crops // LANES, LANES)
    share = functools.partial(call, reads=4 * crops * cols)
    by_proto, by_crop = float(proto_count), float(crop_count)
    sums, norms, mass = share(teacher_kernel, [col_fold, line, whole], gathered, protos)
    held = gathered, protos, norms
    part, scores, spread = share(
        functools.partial(first_row_kernel, by_proto), [row_pair, whole, whole], *held, mass, gather(sums, Z, nz)
    )
    sums, totals = share(functools.partial(first_col_kernel, by_crop), [col_fold, row_fold], mass, gather_head(part))
    (part,) = share(functools.partial(row_kernel, by_proto), [row_fold], mass, gather(sums, Z, nz))
    (sums,) = share(functools.partial(col_kernel, by_crop), [col_fold], mass, gather_head(part))
    part, scale = share(functools.partial(cross_kernel, by_proto), [row_pair, line], mass, scores, gather(sums, Z, nz))
    grad, back, loss = share(
        functools.partial(grad_kernel, by_crop), [(bot, cols), line, (crops_in // LANES, LANES)], *held, mass, spread, scale, gather_head(part), totals,
        scalar=here.astype(jnp.int32).reshape(1),
    )
    wire = lax.all_to_all(grad.astype(jnp.float16).reshape(nz, nx * rows_in, cols), Z, 0, 0, tiled=True)
    total = jnp.sum(wire.astype(jnp.float32), axis=0) * back
    total = lax.all_to_all(total.reshape(nx, rows_in, cols), "x", 0, 0, tiled=True)
    return total.transpose(1, 0, 2).reshape(rows_in, cols_in), loss.reshape(crops_in)


def solution(mesh):
    fine = Mesh(mesh.devices.reshape(4, 4, 4, 4, 2), ("h", "l", "x", "y", "c"))
    return jax.shard_map(
        local,
        mesh=fine,
        in_specs=(P(ZX, None), P(ZX, None), P(ZX, ("y", "c"))),
        out_specs=(P(ZX, ("y", "c")), P(ZX)),
        check_vma=False,
    )
```

```python
import functools

import jax
import jax.numpy as jnp
from jax import lax
from jax.experimental import pallas as pl
from jax.experimental.pallas import tpu as pltpu
from jax.sharding import Mesh, PartitionSpec as P

ITERS = 3
TEACHER_TEMP = 0.04
STUDENT_TEMP = 0.1
WIRE_SCALE = 32.0

Z = "z"
ZX = ("z", "x")
XYC = ("x", "head")


def gather(values, axes, size):
    copies = jnp.broadcast_to(values[None], (size,) + values.shape)
    return lax.all_to_all(copies, axes, 0, 0, tiled=True)


def gather_head(values):
    return gather(values, XYC, 32)


TILE = 256
LANES = 128
VMEM_LIMIT = 16 * 1024 * 1024


def lanes_to_rows(row):
    return jnp.transpose(jnp.broadcast_to(row, (LANES, row.shape[1])))


def row_totals(block):
    part = block[:, :LANES]
    for start in range(LANES, block.shape[1], LANES):
        part = part + block[:, start : start + LANES]
    return jnp.sum(jnp.transpose(part), axis=0, keepdims=True)


def unit_kernel(feat_ref, unit_ref):
    bot = feat_ref.shape[1] // 2
    for half in (slice(0, bot), slice(bot, 2 * bot)):
        widened = feat_ref[:, half].astype(jnp.float32)
        scale = jnp.sqrt(jnp.sum(widened * widened, axis=1, keepdims=True) + 1e-06)
        unit_ref[:, half] = (widened / scale).astype(jnp.bfloat16)


def fold(row):
    return jnp.concatenate([row[:, i : i + LANES] for i in range(0, row.shape[1], LANES)], axis=0)


def unfold(block):
    return jnp.concatenate([block[i : i + 1, :] for i in range(block.shape[0])], axis=1)


def put_totals(held, first, block):
    row = lax.broadcasted_iota(jnp.int32, held.shape, 0)
    for i in range(TILE // LANES):
        held = jnp.where(row == first + i, row_totals(block[i * LANES : (i + 1) * LANES, :]), held)
    return held


def over_tiles(step, ref, rows):
    def body(i, held):
        tile = pl.ds(pl.multiple_of(i * TILE, TILE), TILE)
        return step(i * (TILE // LANES), tile, held)

    return lax.fori_loop(0, ref.shape[0] // TILE, body, jnp.zeros((rows, LANES), jnp.float32), unroll=True)


def masses_of(unit_ref, proto_ref, norm_ref, rows):
    bot = proto_ref.shape[0]
    raw = jnp.dot(unit_ref[rows, :bot], proto_ref[...], preferred_element_type=jnp.float32)
    return jnp.exp(raw * (1.0 / (norm_ref[...] * TEACHER_TEMP)))


def scores_of(unit_ref, proto_ref, norm_ref, rows):
    bot = proto_ref.shape[0]
    raw = jnp.dot(unit_ref[rows, bot:], proto_ref[...], preferred_element_type=jnp.float32)
    return raw * (1.0 / (norm_ref[...] * STUDENT_TEMP))


def teacher_kernel(unit_ref, proto_ref, col_ref, norm_ref, mass_ref):
    widened = proto_ref[...].astype(jnp.float32)
    norm_ref[...] = jnp.sqrt(jnp.sum(widened * widened, axis=0, keepdims=True) + 1e-06)

    def step(i, sums):
        rows = pl.ds(pl.multiple_of(i * TILE, TILE), TILE)
        mass = masses_of(unit_ref, proto_ref, norm_ref, rows)
        mass_ref[rows, :] = mass
        return sums + jnp.sum(mass, axis=0, keepdims=True)

    steps = unit_ref.shape[0] // TILE
    col_ref[...] = fold(lax.fori_loop(0, steps, step, jnp.zeros(norm_ref.shape, jnp.float32), unroll=True))


def first_row_kernel(proto_count, unit_ref, proto_ref, norm_ref, mass_ref, got_ref, out_ref, score_ref, spread_ref):
    scale = unfold(1.0 / (proto_count * jnp.sum(got_ref[...], axis=0)))
    half = out_ref.shape[0] // 2

    def step(first, rows, held):
        scores = scores_of(unit_ref, proto_ref, norm_ref, rows)
        spread = jnp.exp(scores)
        score_ref[rows, :] = scores
        spread_ref[rows, :] = spread
        held = put_totals(held, first, mass_ref[rows, :] * scale)
        return put_totals(held, half + first, spread)

    out_ref[...] = over_tiles(step, mass_ref, 2 * half)


def row_kernel(proto_count, mass_ref, got_ref, out_ref):
    scale = unfold(1.0 / (proto_count * jnp.sum(got_ref[...], axis=0)))

    def step(first, rows, held):
        return put_totals(held, first, mass_ref[rows, :] * scale)

    out_ref[...] = over_tiles(step, mass_ref, out_ref.shape[0])


def col_sums(scale, mass_ref):
    cols = []
    tall = [lanes_to_rows(scale[i : i + 1, :]) for i in range(scale.shape[0])]
    for lane in range(0, mass_ref.shape[1], LANES):
        total = jnp.zeros((1, LANES), jnp.float32)
        for i, factor in enumerate(tall):
            block = mass_ref[i * LANES : (i + 1) * LANES, lane : lane + LANES] * factor
            total = total + jnp.sum(block, axis=0, keepdims=True)
        cols.append(total)
    return jnp.concatenate(cols, axis=0)


def first_col_kernel(crop_count, mass_ref, got_ref, out_ref, total_ref):
    both = jnp.sum(got_ref[...], axis=0)
    half = both.shape[0] // 2
    total_ref[...] = both[half:]
    out_ref[...] = col_sums(1.0 / (crop_count * both[:half]), mass_ref)


def col_kernel(crop_count, mass_ref, got_ref, out_ref):
    out_ref[...] = col_sums(1.0 / (crop_count * jnp.sum(got_ref[...], axis=0)), mass_ref)


def cross_kernel(proto_count, mass_ref, score_ref, got_ref, out_ref, scale_ref):
    scale = unfold(1.0 / (proto_count * jnp.sum(got_ref[...], axis=0)))
    scale_ref[...] = scale
    half = out_ref.shape[0] // 2

    def step(first, rows, held):
        weighted = mass_ref[rows, :] * scale
        held = put_totals(held, first, weighted)
        return put_totals(held, half + first, weighted * score_ref[rows, :])

    out_ref[...] = over_tiles(step, mass_ref, 2 * half)


def grad_kernel(crop_count, here_ref, unit_ref, proto_ref, norm_ref, mass_ref, spread_ref, scale_ref, got_ref, total_ref, out_ref, back_ref, loss_ref):
    sums = jnp.sum(got_ref[...], axis=0)
    totals = total_ref[...]
    half = totals.shape[0]
    losses = jnp.log(totals) - sums[half:] / sums[:half]
    block = loss_ref.shape[0]
    loss = losses[:block]
    for x in range(1, half // block):
        loss = jnp.where(here_ref[0] == x, losses[x * block : (x + 1) * block], loss)
    loss_ref[...] = loss
    bot = proto_ref.shape[0]
    by_row = 1.0 / sums[:half]
    by_total = 1.0 / totals
    grad = jnp.zeros(out_ref.shape, jnp.float32)
    for start in range(0, mass_ref.shape[0], TILE):
        tiles = []
        for top in range(start, start + TILE, LANES):
            rows, i = slice(top, top + LANES), top // LANES
            tall_total = lanes_to_rows(by_total[i : i + 1, :])
            tall_row = lanes_to_rows(by_row[i : i + 1, :])
            pieces = []
            for lane in range(0, mass_ref.shape[1], LANES):
                cols = slice(lane, lane + LANES)
                target = mass_ref[rows, cols] * scale_ref[:, cols] * tall_row
                pieces.append((spread_ref[rows, cols] * tall_total - target).astype(jnp.bfloat16))
            tiles.append(jnp.concatenate(pieces, axis=1))
        grad = grad + lax.dot_general(
            unit_ref[start : start + TILE, bot:], jnp.concatenate(tiles, axis=0),
            (((0,), (0,)), ((), ())), preferred_element_type=jnp.float32,
        )
    normed = proto_ref[...].astype(jnp.float32) / norm_ref[...]
    dots = jnp.sum(normed * grad, axis=0, keepdims=True)
    out_ref[...] = (grad - normed * dots) * WIRE_SCALE
    back_ref[...] = 1.0 / (norm_ref[...] * (WIRE_SCALE * STUDENT_TEMP * crop_count))


def call(kernel, outs, *args, reads, scalar=None, dtype=jnp.float32):
    vmem = pl.BlockSpec(memory_space=pltpu.VMEM)
    specs = [vmem] * len(args)
    if scalar is not None:
        args, specs = (scalar,) + args, [pl.BlockSpec(memory_space=pltpu.SMEM)] + specs
    return pl.pallas_call(
        kernel,
        out_shape=[jax.ShapeDtypeStruct(shape, dtype) for shape in outs],
        in_specs=specs,
        out_specs=[vmem] * len(outs),
        compiler_params=pltpu.CompilerParams(vmem_limit_bytes=VMEM_LIMIT),
        cost_estimate=pl.CostEstimate(flops=reads, bytes_accessed=reads, transcendentals=0),
    )(*args)


def local(teacher_feat, student_feat, proto_v):
    rows_in, cols_in = proto_v.shape
    nx = lax.axis_size("x")
    nz = lax.axis_size("z")
    cols = cols_in // nx
    crop_count = teacher_feat.shape[0] * nz * nx
    proto_count = cols * 32

    crops_in, bot = teacher_feat.shape
    here = lax.axis_index("x")
    feats = jnp.concatenate([teacher_feat, student_feat], axis=1)
    (units,) = call(unit_kernel, [feats.shape], feats, reads=4 * crops_in * bot, dtype=jnp.bfloat16)
    gathered = jnp.zeros((nx * crops_in, 2 * bot), units.dtype)
    for step in range(nx):
        block = lax.ppermute(units, "x", [((i + step) % nx, i) for i in range(nx)]) if step else units
        gathered = lax.dynamic_update_slice(gathered, block, ((here + step) % nx * crops_in, 0))

    quarters = proto_v.reshape(rows_in, nx, cols).transpose(1, 0, 2)
    quarters = lax.all_to_all(quarters, "x", 0, 0, tiled=True).reshape(nx * rows_in, cols)
    protos = gather(quarters, Z, nz).reshape(bot, cols)

    crops = nx * crops_in
    whole, line = (crops, cols), (1, cols)
    col_fold, row_fold, row_pair = (cols // LANES, LANES), (crops // LANES, LANES), (2 * crops // LANES, LANES)
    share = functools.partial(call, reads=4 * crops * cols)
    by_proto, by_crop = float(proto_count), float(crop_count)
    sums, norms, mass = share(teacher_kernel, [col_fold, line, whole], gathered, protos)
    held = gathered, protos, norms
    part, scores, spread = share(
        functools.partial(first_row_kernel, by_proto), [row_pair, whole, whole], *held, mass, gather(sums, Z, nz)
    )
    sums, totals = share(functools.partial(first_col_kernel, by_crop), [col_fold, row_fold], mass, gather_head(part))
    (part,) = share(functools.partial(row_kernel, by_proto), [row_fold], mass, gather(sums, Z, nz))
    (sums,) = share(functools.partial(col_kernel, by_crop), [col_fold], mass, gather_head(part))
    part, scale = share(functools.partial(cross_kernel, by_proto), [row_pair, line], mass, scores, gather(sums, Z, nz))
    grad, back, loss = share(
        functools.partial(grad_kernel, by_crop), [(bot, cols), line, (crops_in // LANES, LANES)], *held, mass, spread, scale, gather_head(part), totals,
        scalar=here.astype(jnp.int32).reshape(1),
    )
    wire = lax.all_to_all(grad.astype(jnp.float16).reshape(nz, nx * rows_in, cols), Z, 0, 0, tiled=True)
    total = jnp.sum(wire.astype(jnp.float32), axis=0) * back
    total = lax.all_to_all(total.reshape(nx, rows_in, cols), "x", 0, 0, tiled=True)
    return total.transpose(1, 0, 2).reshape(rows_in, cols_in), loss.reshape(crops_in)


def solution(mesh):
    fine = Mesh(mesh.devices.reshape(16, 4, 8), ("z", "x", "head"))
    return jax.shard_map(
        local,
        mesh=fine,
        in_specs=(P(ZX, None), P(ZX, None), P(ZX, "head")),
        out_specs=(P(ZX, "head"), P(ZX)),
        check_vma=False,
    )
```

```python
import functools

import jax
import jax.numpy as jnp
from jax import lax
from jax.experimental import pallas as pl
from jax.experimental.pallas import tpu as pltpu
from jax.sharding import Mesh, PartitionSpec as P

ITERS = 3
TEACHER_TEMP = 0.04
STUDENT_TEMP = 0.1
WIRE_SCALE = 32.0

Z = "z"
ZX = ("z", "x")
XYC = ("x", "head")


def gather(values, axes, size):
    copies = jnp.broadcast_to(values[None], (size,) + values.shape)
    return lax.all_to_all(copies, axes, 0, 0, tiled=True)


def gather_head(values):
    return gather(values, XYC, 32)


TILE = 256
LANES = 128
VMEM_LIMIT = 16 * 1024 * 1024


def lanes_to_rows(row):
    return jnp.transpose(jnp.broadcast_to(row, (LANES, row.shape[1])))


def row_totals(block):
    part = block[:, :LANES]
    for start in range(LANES, block.shape[1], LANES):
        part = part + block[:, start : start + LANES]
    return jnp.sum(jnp.transpose(part), axis=0, keepdims=True)


def unit_kernel(feat_ref, unit_ref):
    bot = feat_ref.shape[1] // 2
    for half in (slice(0, bot), slice(bot, 2 * bot)):
        widened = feat_ref[:, half].astype(jnp.float32)
        scale = jnp.sqrt(jnp.sum(widened * widened, axis=1, keepdims=True) + 1e-06)
        unit_ref[:, half] = (widened / scale).astype(jnp.bfloat16)


def fold(row):
    return jnp.concatenate([row[:, i : i + LANES] for i in range(0, row.shape[1], LANES)], axis=0)


def unfold(block):
    return jnp.concatenate([block[i : i + 1, :] for i in range(block.shape[0])], axis=1)


def put_totals(held, first, block):
    row = lax.broadcasted_iota(jnp.int32, held.shape, 0)
    for i in range(TILE // LANES):
        held = jnp.where(row == first + i, row_totals(block[i * LANES : (i + 1) * LANES, :]), held)
    return held


def over_tiles(step, ref, rows):
    def body(i, held):
        tile = pl.ds(pl.multiple_of(i * TILE, TILE), TILE)
        return step(i * (TILE // LANES), tile, held)

    return lax.fori_loop(0, ref.shape[0] // TILE, body, jnp.zeros((rows, LANES), jnp.float32), unroll=True)


def masses_of(unit_ref, proto_ref, norm_ref, rows):
    bot = proto_ref.shape[0]
    raw = jnp.dot(unit_ref[rows, :bot], proto_ref[...], preferred_element_type=jnp.float32)
    return jnp.exp(raw * (1.0 / (norm_ref[...] * TEACHER_TEMP)))


def scores_of(unit_ref, proto_ref, norm_ref, rows):
    bot = proto_ref.shape[0]
    raw = jnp.dot(unit_ref[rows, bot:], proto_ref[...], preferred_element_type=jnp.float32)
    return raw * (1.0 / (norm_ref[...] * STUDENT_TEMP))


def teacher_kernel(unit_ref, proto_ref, col_ref, norm_ref, mass_ref):
    widened = proto_ref[...].astype(jnp.float32)
    norm_ref[...] = jnp.sqrt(jnp.sum(widened * widened, axis=0, keepdims=True) + 1e-06)

    def step(i, sums):
        rows = pl.ds(pl.multiple_of(i * TILE, TILE), TILE)
        mass = masses_of(unit_ref, proto_ref, norm_ref, rows)
        mass_ref[rows, :] = mass
        return sums + jnp.sum(mass, axis=0, keepdims=True)

    steps = unit_ref.shape[0] // TILE
    col_ref[...] = fold(lax.fori_loop(0, steps, step, jnp.zeros(norm_ref.shape, jnp.float32), unroll=True))


def first_row_kernel(proto_count, unit_ref, proto_ref, norm_ref, mass_ref, got_ref, out_ref, score_ref, spread_ref):
    scale = unfold(1.0 / (proto_count * jnp.sum(got_ref[...].astype(jnp.float32), axis=0)))
    half = out_ref.shape[0] // 2

    def step(first, rows, held):
        scores = scores_of(unit_ref, proto_ref, norm_ref, rows)
        spread = jnp.exp(scores)
        score_ref[rows, :] = scores
        spread_ref[rows, :] = spread
        held = put_totals(held, first, mass_ref[rows, :] * scale)
        return put_totals(held, half + first, spread)

    out_ref[...] = over_tiles(step, mass_ref, 2 * half)


def row_kernel(proto_count, mass_ref, got_ref, out_ref):
    scale = unfold(1.0 / (proto_count * jnp.sum(got_ref[...].astype(jnp.float32), axis=0)))

    def step(first, rows, held):
        return put_totals(held, first, mass_ref[rows, :] * scale)

    out_ref[...] = over_tiles(step, mass_ref, out_ref.shape[0])


def col_sums(scale, mass_ref):
    cols = []
    tall = [lanes_to_rows(scale[i : i + 1, :]) for i in range(scale.shape[0])]
    for lane in range(0, mass_ref.shape[1], LANES):
        total = jnp.zeros((1, LANES), jnp.float32)
        for i, factor in enumerate(tall):
            block = mass_ref[i * LANES : (i + 1) * LANES, lane : lane + LANES] * factor
            total = total + jnp.sum(block, axis=0, keepdims=True)
        cols.append(total)
    return jnp.concatenate(cols, axis=0)


def first_col_kernel(crop_count, mass_ref, got_ref, out_ref, total_ref):
    both = jnp.sum(got_ref[...].astype(jnp.float32), axis=0)
    half = both.shape[0] // 2
    total_ref[...] = both[half:]
    out_ref[...] = col_sums(1.0 / (crop_count * both[:half]), mass_ref)


def col_kernel(crop_count, mass_ref, got_ref, out_ref):
    out_ref[...] = col_sums(1.0 / (crop_count * jnp.sum(got_ref[...].astype(jnp.float32), axis=0)), mass_ref)


def cross_kernel(proto_count, mass_ref, score_ref, got_ref, out_ref, scale_ref):
    scale = unfold(1.0 / (proto_count * jnp.sum(got_ref[...].astype(jnp.float32), axis=0)))
    scale_ref[...] = scale
    half = out_ref.shape[0] // 2

    def step(first, rows, held):
        weighted = mass_ref[rows, :] * scale
        held = put_totals(held, first, weighted)
        return put_totals(held, half + first, weighted * score_ref[rows, :])

    out_ref[...] = over_tiles(step, mass_ref, 2 * half)


def grad_kernel(crop_count, here_ref, unit_ref, proto_ref, norm_ref, mass_ref, spread_ref, scale_ref, got_ref, total_ref, out_ref, back_ref, loss_ref):
    sums = jnp.sum(got_ref[...].astype(jnp.float32), axis=0)
    totals = total_ref[...]
    half = totals.shape[0]
    losses = jnp.log(totals) - sums[half:] / sums[:half]
    block = loss_ref.shape[0]
    loss = losses[:block]
    for x in range(1, half // block):
        loss = jnp.where(here_ref[0] == x, losses[x * block : (x + 1) * block], loss)
    loss_ref[...] = loss
    bot = proto_ref.shape[0]
    by_row = 1.0 / sums[:half]
    by_total = 1.0 / totals
    grad = jnp.zeros(out_ref.shape, jnp.float32)
    for start in range(0, mass_ref.shape[0], TILE):
        tiles = []
        for top in range(start, start + TILE, LANES):
            rows, i = slice(top, top + LANES), top // LANES
            tall_total = lanes_to_rows(by_total[i : i + 1, :])
            tall_row = lanes_to_rows(by_row[i : i + 1, :])
            pieces = []
            for lane in range(0, mass_ref.shape[1], LANES):
                cols = slice(lane, lane + LANES)
                target = mass_ref[rows, cols] * scale_ref[:, cols] * tall_row
                pieces.append((spread_ref[rows, cols] * tall_total - target).astype(jnp.bfloat16))
            tiles.append(jnp.concatenate(pieces, axis=1))
        grad = grad + lax.dot_general(
            unit_ref[start : start + TILE, bot:], jnp.concatenate(tiles, axis=0),
            (((0,), (0,)), ((), ())), preferred_element_type=jnp.float32,
        )
    normed = proto_ref[...].astype(jnp.float32) / norm_ref[...]
    dots = jnp.sum(normed * grad, axis=0, keepdims=True)
    out_ref[...] = (grad - normed * dots) * WIRE_SCALE
    back_ref[...] = 1.0 / (norm_ref[...] * (WIRE_SCALE * STUDENT_TEMP * crop_count))


def call(kernel, outs, *args, reads, scalar=None, dtype=jnp.float32):
    vmem = pl.BlockSpec(memory_space=pltpu.VMEM)
    specs = [vmem] * len(args)
    if scalar is not None:
        args, specs = (scalar,) + args, [pl.BlockSpec(memory_space=pltpu.SMEM)] + specs
    return pl.pallas_call(
        kernel,
        out_shape=[jax.ShapeDtypeStruct(shape, dtype) for shape in outs],
        in_specs=specs,
        out_specs=[vmem] * len(outs),
        compiler_params=pltpu.CompilerParams(vmem_limit_bytes=VMEM_LIMIT),
        cost_estimate=pl.CostEstimate(flops=reads, bytes_accessed=reads, transcendentals=0),
    )(*args)


def local(teacher_feat, student_feat, proto_v):
    rows_in, cols_in = proto_v.shape
    nx = lax.axis_size("x")
    nz = lax.axis_size("z")
    cols = cols_in // nx
    crop_count = teacher_feat.shape[0] * nz * nx
    proto_count = cols * 32

    crops_in, bot = teacher_feat.shape
    here = lax.axis_index("x")
    feats = jnp.concatenate([teacher_feat, student_feat], axis=1)
    (units,) = call(unit_kernel, [feats.shape], feats, reads=4 * crops_in * bot, dtype=jnp.bfloat16)
    gathered = jnp.zeros((nx * crops_in, 2 * bot), units.dtype)
    for step in range(nx):
        block = lax.ppermute(units, "x", [((i + step) % nx, i) for i in range(nx)]) if step else units
        gathered = lax.dynamic_update_slice(gathered, block, ((here + step) % nx * crops_in, 0))

    quarters = proto_v.reshape(rows_in, nx, cols).transpose(1, 0, 2)
    quarters = lax.all_to_all(quarters, "x", 0, 0, tiled=True).reshape(nx * rows_in, cols)
    protos = gather(quarters, Z, nz).reshape(bot, cols)

    crops = nx * crops_in
    whole, line = (crops, cols), (1, cols)
    col_fold, row_fold, row_pair = (cols // LANES, LANES), (crops // LANES, LANES), (2 * crops // LANES, LANES)
    share = functools.partial(call, reads=4 * crops * cols)
    by_proto, by_crop = float(proto_count), float(crop_count)
    sums, norms, mass = share(teacher_kernel, [col_fold, line, whole], gathered, protos)
    held = gathered, protos, norms
    part, scores, spread = share(
        functools.partial(first_row_kernel, by_proto), [row_pair, whole, whole], *held, mass, gather(sums.astype(jnp.bfloat16), Z, nz)
    )
    sums, totals = share(functools.partial(first_col_kernel, by_crop), [col_fold, row_fold], mass, gather_head(part))
    (part,) = share(functools.partial(row_kernel, by_proto), [row_fold], mass, gather(sums.astype(jnp.bfloat16), Z, nz))
    (sums,) = share(functools.partial(col_kernel, by_crop), [col_fold], mass, gather_head(part))
    part, scale = share(functools.partial(cross_kernel, by_proto), [row_pair, line], mass, scores, gather(sums, Z, nz))
    grad, back, loss = share(
        functools.partial(grad_kernel, by_crop), [(bot, cols), line, (crops_in // LANES, LANES)], *held, mass, spread, scale, gather_head(part), totals,
        scalar=here.astype(jnp.int32).reshape(1),
    )
    wire = lax.all_to_all(grad.astype(jnp.float16).reshape(nz, nx * rows_in, cols), Z, 0, 0, tiled=True)
    total = jnp.sum(wire.astype(jnp.float32), axis=0) * back
    total = lax.all_to_all(total.reshape(nx, rows_in, cols), "x", 0, 0, tiled=True)
    return total.transpose(1, 0, 2).reshape(rows_in, cols_in), loss.reshape(crops_in)


def solution(mesh):
    fine = Mesh(mesh.devices.reshape(16, 4, 8), ("z", "x", "head"))
    return jax.shard_map(
        local,
        mesh=fine,
        in_specs=(P(ZX, None), P(ZX, None), P(ZX, "head")),
        out_specs=(P(ZX, "head"), P(ZX)),
        check_vma=False,
    )
```
